768 devices in a mesh: outer: 48 (over y_lo, z, core), ep: 4 (over x), tp: 4 (over y_hi).
Axes of the slice: x: 4, y: 8 (y_hi: 4, y_lo: 2; y = y_hi * 2 + y_lo), z: 12, core: 2. Of those that a mesh axis runs over, the one named last changes fastest.
Arguments:
- unnormed_queries: bfloat16 [24576, 8192], P(('outer', 'ep'), 'tp'), may hold values from -100 to 100
- unnormed_keys: bfloat16 [24576, 512], P(('outer', 'ep'), 'tp'), may hold values from -100 to 100
- value: bfloat16 [24576, 512], P(('outer', 'ep'), 'tp'), may hold values from -6 to 6
- output_gradient: bfloat16 [24576, 8192], P(('outer', 'ep'), 'tp'), may hold values from -80 to 80
- segment_ids: int32 [24576], P(('outer', 'ep')), may hold values from 0 to 53, never falling along the last dimension, each value on 1 to 896 neighbouring positions
- query_norm_gain: float32 [128], replicated, may hold values from 0.5 to 5.5
- key_norm_gain: float32 [128], replicated, may hold values from 0.5 to 5.5
Outputs:
- query_grad: bfloat16 [24576, 8192], P(('outer', 'ep'), 'tp')
- raw_key_gradient: bfloat16 [24576, 512], P(('outer', 'ep'), 'tp')
- value_gradient: bfloat16 [24576, 512], P(('outer', 'ep'), 'tp')
- query_gain_grad: float32 [128], replicated
- key_gain_grad: float32 [128], replicated
The draws below stay inside these ranges and needn't reach their ends.
Inputs may be any that keep to these rules, and one draw needn't show every extreme that they name: `segment_ids`: document numbers never fall along the tokens; each document holds at most 896 tokens, and one holds exactly 896.
All inputs are finite; a program needn't handle non-finite values.
Results may differ from the reference program's by a relative error of at most 0.0095.
The reference program's roundings to bfloat16 on the way count: a program that leaves them out, or rounds other values in their place, can miss the bound.
Values may be sent and summed in bfloat16 or wider, within the bound.
No kernel may reach another device: no remote copies, remote signals or barrier semaphores. Data moves between devices by JAX's collectives and lax.ppermute only.
A program may use at most 64 MiB of HBM per device.

```python
import math
import jax
import jax.numpy as jnp
import numpy as np
from jax import lax

QUERY_HEADS = 64
KEY_VALUE_HEADS = 4
HEAD_SIZE = 128
TOK_DEV = 128
PACKED_TOKENS = 24576
SPAN = 8
SEG_MOST = 896


def shared_keys(key):
    base_offset = jax.random.normal(key, (PACKED_TOKENS, KEY_VALUE_HEADS, HEAD_SIZE), jnp.float32)
    return base_offset


def scale_per_row(key, shape):
    return jnp.exp(jax.random.uniform(key, shape, jnp.float32, 0.0, math.log(10.0)))


def draw_unnormed_keys(key, part):
    shared_heads = shared_keys(key)
    key = jax.random.fold_in(key, 1)
    scaled_input = shared_heads * scale_per_row(key, (PACKED_TOKENS, KEY_VALUE_HEADS, 1))
    return scaled_input.reshape(PACKED_TOKENS, KEY_VALUE_HEADS * HEAD_SIZE).astype(jnp.bfloat16)


def draw_unnormed_queries(key, part):
    query_groups = QUERY_HEADS // KEY_VALUE_HEADS
    key = jax.random.fold_in(key, 2)
    fresh_draws = jax.random.normal(key, (PACKED_TOKENS, KEY_VALUE_HEADS, query_groups, HEAD_SIZE), jnp.float32)
    mixed_input = fresh_draws
    scaled_input = mixed_input * scale_per_row(jax.random.fold_in(key, 5), (PACKED_TOKENS, KEY_VALUE_HEADS, query_groups, 1))
    return scaled_input.reshape(PACKED_TOKENS, QUERY_HEADS * HEAD_SIZE).astype(jnp.bfloat16)


def draw_query_norm_gain(key, part):
    key = jax.random.fold_in(key, 3)
    return jax.random.uniform(key, (HEAD_SIZE,), jnp.float32, 0.5, 1.5)


def draw_key_norm_gain(key, part):
    key = jax.random.fold_in(key, 4)
    return jax.random.uniform(key, (HEAD_SIZE,), jnp.float32, 0.5, 1.5)


def draw_output_gradient(key, part):
    key = jax.random.fold_in(key, 6)
    rise_rows = 1.0 + 2.0 * jnp.arange(PACKED_TOKENS, dtype=jnp.float32)[:, None] / (PACKED_TOKENS - 1)
    head_index = (jnp.arange(QUERY_HEADS * HEAD_SIZE) // HEAD_SIZE).astype(jnp.float32)[None, :]
    rise_cols = 1.0 + 2.0 * head_index / max(QUERY_HEADS - 1, 1)
    normal_part = jax.random.normal(key, (PACKED_TOKENS, QUERY_HEADS * HEAD_SIZE), jnp.float32)
    return (normal_part * rise_rows * rise_cols).astype(jnp.bfloat16)


def levels(key, dims, pieces, low, high):
    factor_of, own = 1.0, jax.random.fold_in(key, 6)
    for position, parts in pieces:
        steps = jnp.exp(jax.random.uniform(jax.random.fold_in(own, position), (parts,), jnp.float32, low / len(pieces), high / len(pieces)))
        factor_of = factor_of * jnp.repeat(steps, dims[position] // parts).reshape([-1 if axis == position else 1 for axis in range(len(dims))])
    return factor_of


def profile(count, total, reach, skew):
    portions = [(1 << 20) // math.isqrt(grade ** skew) + 1 for grade in range(2, count + 1)]
    surplus, holding = total - reach - (count - 1), [1] * (count - 1)
    while surplus > 0:
        free = [i for i in range(count - 1) if holding[i] < reach]
        mass, budget = sum([portions[i] for i in free]), surplus
        for i in free:
            more = min(reach - holding[i], max(1, budget * portions[i] // mass), surplus)
            holding[i] = holding[i] + more
            surplus = surplus - more
    return np.array([reach] + holding)


def ragged(stream_key, count, total, limit, skew):
    if count == 2:
        one = jax.random.randint(stream_key, (), max(1, total - limit), min(limit, total - 1) + 1)
        return jnp.stack([one, total - one])
    lengths = jnp.asarray(profile(count, total, limit, skew), jnp.int32)
    pairs = (count - 1) // 2
    donor, sink = lengths[1:1 + 2 * pairs:2], lengths[2:2 + 2 * pairs:2]
    slack = jnp.minimum(donor - 1, limit - sink)
    moved = jax.random.randint(jax.random.fold_in(stream_key, 1), (pairs,), 0, 1 << 20) % (slack + 1)
    lengths = lengths.at[1:1 + 2 * pairs:2].set(donor - moved).at[2:2 + 2 * pairs:2].set(sink + moved)
    return lengths[jax.random.permutation(jax.random.fold_in(stream_key, 2), count)]


def gaussian(rng, dims, deviation, bound, pieces=(), kind=jnp.bfloat16):
    loudness = levels(rng, dims, pieces, -0.22, 0.18) if pieces else 1.0
    entries = jax.random.normal(rng, dims, jnp.float32) * deviation * loudness
    return jnp.minimum(jnp.maximum(entries, -bound), bound).astype(kind)


def setup_inputs(seed: int = 0) -> dict:
    streams_of = jax.random.split(jax.random.key(seed), 8)
    unnormed_queries = draw_unnormed_queries(jax.random.fold_in(streams_of[7], 71), 0)
    unnormed_keys = draw_unnormed_keys(jax.random.fold_in(streams_of[7], 71), 0)
    value = gaussian(streams_of[2], (PACKED_TOKENS, KEY_VALUE_HEADS * HEAD_SIZE), 1.0, 6.0, ((0, 192), (1, 4)))
    output_gradient = draw_output_gradient(jax.random.fold_in(streams_of[7], 71), 0)
    segment_ids = jnp.searchsorted(jnp.cumsum(ragged(streams_of[4], 2 * PACKED_TOKENS // SEG_MOST, PACKED_TOKENS, SEG_MOST, 2)), jnp.arange(PACKED_TOKENS), side="right").astype(jnp.int32)
    query_norm_gain = draw_query_norm_gain(jax.random.fold_in(streams_of[7], 71), 0)
    key_norm_gain = draw_key_norm_gain(jax.random.fold_in(streams_of[7], 71), 0)
    return dict(unnormed_queries=unnormed_queries, unnormed_keys=unnormed_keys, value=value, output_gradient=output_gradient, segment_ids=segment_ids, query_norm_gain=query_norm_gain, key_norm_gain=key_norm_gain)


EPS = 1e-06
NEG = -1e+30

def head_rms_norm(raw, gain):
    value_rows = raw.astype(jnp.float32)
    inverse = lax.rsqrt(lax.optimization_barrier(jnp.mean(value_rows * value_rows, axis=-1, keepdims=True)) + EPS)
    unit = value_rows * inverse
    return (unit, inverse, (unit * gain).astype(jnp.bfloat16))

def norm_backward(grad, unit, inverse, gain):
    scaled_input = grad * gain
    inner = lax.optimization_barrier(jnp.mean(scaled_input * unit, axis=-1, keepdims=True))
    return inverse * (scaled_input - unit * inner)

def reference(unnormed_queries, unnormed_keys, value, output_gradient, segment_ids, query_norm_gain, key_norm_gain):
    query_groups = QUERY_HEADS // KEY_VALUE_HEADS
    scale = 1.0 / math.sqrt(HEAD_SIZE)
    blocks = PACKED_TOKENS // TOK_DEV
    error_margin = (SPAN - 1) * TOK_DEV
    window = SPAN * TOK_DEV
    unit_queries, query_inverse_norm, normed_queries = head_rms_norm(unnormed_queries.reshape(PACKED_TOKENS, KEY_VALUE_HEADS, query_groups, HEAD_SIZE), query_norm_gain)
    unit_keys, key_inverse_norm, normed_keys = head_rms_norm(unnormed_keys.reshape(PACKED_TOKENS, KEY_VALUE_HEADS, HEAD_SIZE), key_norm_gain)
    value_rows = value.reshape(PACKED_TOKENS, KEY_VALUE_HEADS, HEAD_SIZE)
    gradient_list = output_gradient.reshape(PACKED_TOKENS, KEY_VALUE_HEADS, query_groups, HEAD_SIZE)
    padded_keys = jnp.concatenate([jnp.zeros((error_margin, KEY_VALUE_HEADS, HEAD_SIZE), jnp.bfloat16), normed_keys], 0)
    padded_values = jnp.concatenate([jnp.zeros((error_margin, KEY_VALUE_HEADS, HEAD_SIZE), jnp.bfloat16), value_rows], 0)
    seg_pad = jnp.concatenate([jnp.full((error_margin,), -1, jnp.int32), segment_ids.astype(jnp.int32)], 0)

    def step(carry, index):
        key_acc, value_acc = carry
        start = (index * TOK_DEV).astype(jnp.int32)
        q_blk = lax.dynamic_slice_in_dim(normed_queries, start, TOK_DEV, 0).astype(jnp.float32)
        g_blk = lax.dynamic_slice_in_dim(gradient_list, start, TOK_DEV, 0).astype(jnp.float32)
        seg_q = lax.dynamic_slice_in_dim(segment_ids.astype(jnp.int32), start, TOK_DEV, 0)
        k_win = lax.dynamic_slice_in_dim(padded_keys, start, window, 0).astype(jnp.float32)
        v_win = lax.dynamic_slice_in_dim(padded_values, start, window, 0).astype(jnp.float32)
        seg_k = lax.dynamic_slice_in_dim(seg_pad, start, window, 0)
        q_pos = start + jnp.arange(TOK_DEV, dtype=jnp.int32)
        k_pos = start - error_margin + jnp.arange(window, dtype=jnp.int32)
        live = (seg_q[:, None] == seg_k[None, :]) & (k_pos[None, :] <= q_pos[:, None])
        scores = jnp.einsum('qhgd,khd->hgqk', q_blk, k_win) * scale
        scores = jnp.where(live, scores, NEG)
        top = lax.optimization_barrier(jnp.max(scores, axis=-1, keepdims=True))
        expo = jnp.exp(scores - top)
        probs = expo / lax.optimization_barrier(jnp.sum(expo, axis=-1, keepdims=True))
        probs_b = lax.optimization_barrier(probs.astype(jnp.bfloat16)).astype(jnp.float32)
        attn = jnp.einsum('hgqk,khd->qhgd', probs_b, v_win)
        delta = jnp.transpose(lax.optimization_barrier(jnp.sum(g_blk * attn, axis=-1)), (1, 2, 0))[..., None]
        dv_win = jnp.einsum('hgqk,qhgd->khd', probs_b, g_blk)
        dprob = jnp.einsum('qhgd,khd->hgqk', g_blk, v_win)
        dscore = lax.optimization_barrier((probs * (dprob - delta)).astype(jnp.bfloat16)).astype(jnp.float32)
        dq_blk = jnp.einsum('hgqk,khd->qhgd', dscore, k_win) * scale
        dk_win = jnp.einsum('hgqk,qhgd->khd', dscore, q_blk) * scale
        key_acc = lax.dynamic_update_slice_in_dim(key_acc, lax.dynamic_slice_in_dim(key_acc, start, window, 0) + dk_win, start, 0)
        value_acc = lax.dynamic_update_slice_in_dim(value_acc, lax.dynamic_slice_in_dim(value_acc, start, window, 0) + dv_win, start, 0)
        return ((key_acc, value_acc), dq_blk)
    empty_blocks = jnp.zeros((PACKED_TOKENS + error_margin, KEY_VALUE_HEADS, HEAD_SIZE), jnp.float32)
    (key_acc, value_acc), query_gradient_blocks = lax.scan(step, (empty_blocks, empty_blocks), jnp.arange(blocks, dtype=jnp.int32))
    normed_query_gradient = query_gradient_blocks.reshape(PACKED_TOKENS, KEY_VALUE_HEADS, query_groups, HEAD_SIZE)
    normed_key_gradient = key_acc[error_margin:]
    value_gradient_total = value_acc[error_margin:]
    query_grad = norm_backward(normed_query_gradient, unit_queries, query_inverse_norm, query_norm_gain).astype(jnp.bfloat16).reshape(PACKED_TOKENS, QUERY_HEADS * HEAD_SIZE)
    raw_key_gradient = norm_backward(normed_key_gradient, unit_keys, key_inverse_norm, key_norm_gain).astype(jnp.bfloat16).reshape(PACKED_TOKENS, KEY_VALUE_HEADS * HEAD_SIZE)
    value_gradient = value_gradient_total.astype(jnp.bfloat16).reshape(PACKED_TOKENS, KEY_VALUE_HEADS * HEAD_SIZE)
    factor = 1.0 / math.sqrt(PACKED_TOKENS * QUERY_HEADS)
    query_gain_grad = lax.optimization_barrier(jnp.sum(normed_query_gradient * unit_queries, axis=(0, 1, 2))) * factor
    key_gain_grad = lax.optimization_barrier(jnp.sum(normed_key_gradient * unit_keys, axis=(0, 1))) * factor
    return (query_grad, raw_key_gradient, value_gradient, query_gain_grad, key_gain_grad)
```

```python
import math

import jax
import jax.numpy as jnp
from jax import lax
from jax.experimental import pallas as pl
from jax.experimental.pallas import tpu as pltpu
from jax.sharding import Mesh
from jax.sharding import PartitionSpec as P

HEAD_SIZE = 128
ROWS = 128
SPAN = 8
HEADS = 16
PAIRS = 2
TOKENS = SPAN * ROWS
EXTRA = 16
CHUNK = 2 * ROWS + EXTRA
EPS = 1e-06
NEG = -1e30
SCALE = 1.0 / math.sqrt(HEAD_SIZE)
EXP2_SCALE = SCALE * math.log2(math.e)

SEQ = ("yl", "z", "core", "ep")
ROW = ("core", "ep")
REST = ("yl", "z", "tp")
F32 = jnp.float32
BF16 = jnp.bfloat16


def dot_nt(a, b):
    return lax.dot_general(a, b, (((1,), (1,)), ((), ())), preferred_element_type=F32)


def dot_nn(a, b):
    return lax.dot_general(a, b, (((1,), (0,)), ((), ())), preferred_element_type=F32)


def unit_of(raw):
    inverse = lax.rsqrt(jnp.mean(raw * raw, axis=-1, keepdims=True) + EPS)
    return raw * inverse, inverse


def norm_backward(grad, unit, inverse, gain):
    scaled = grad * gain
    inner = jnp.mean(scaled * unit, axis=-1, keepdims=True)
    return inverse * (scaled - unit * inner)


def fold(x):
    return jnp.sum(x.reshape(x.shape[0] // 8, 8, x.shape[1]), axis=0)


def split(x):
    high = x.astype(BF16)
    return high, (x - high.astype(F32)).astype(BF16)


def attention_kernel(
    here_ref, q_ref, g_ref, win_ref, seg_ref, qgain_ref, kgain_ref,
    qgrad_ref, parts_ref,
    kn, knt, bias, scores, dprob, probs_b, dscore, dk, dv, qsum,
):
    step = pl.program_id(0)
    qgain = qgain_ref[...]
    kgain = kgain_ref[...]

    @pl.when(step == 0)
    def _():
        here = here_ref[0]
        key_row = lax.broadcasted_iota(jnp.int32, (ROWS, ROWS), 0)
        query_col = lax.broadcasted_iota(jnp.int32, (ROWS, ROWS), 1)
        seg_q = jnp.broadcast_to(seg_ref[...].astype(F32), (ROWS, ROWS))
        for p in range(SPAN):
            rows = slice(p * ROWS, (p + 1) * ROWS)
            unit, _ = unit_of(win_ref[p, :ROWS, :].astype(F32))
            normed = (unit * kgain).astype(BF16)
            kn[rows, :] = normed
            knt[:, rows] = (unit * kgain).T.astype(BF16)
            marks = win_ref[p, 2 * ROWS : 2 * ROWS + EXTRA, :].astype(F32)[0:1, :]
            seg_k = jnp.broadcast_to(marks, (ROWS, ROWS)).T
            late = jnp.where(here == p, 1, 0) * key_row > query_col
            hidden = jnp.logical_or(seg_k != seg_q, late)
            bias[rows, :] = jnp.where(hidden, NEG, 0.0)
        dk[...] = jnp.zeros_like(dk)
        dv[...] = jnp.zeros_like(dv)
        qsum[...] = jnp.zeros_like(qsum)

    for pair in range(PAIRS):
        columns = [slice((2 * pair + h) * HEAD_SIZE, (2 * pair + h + 1) * HEAD_SIZE) for h in (0, 1)]
        units = [unit_of(q_ref[:, c].astype(F32)) for c in columns]
        normed = jnp.concatenate([(u * qgain).astype(BF16) for u, _ in units], axis=0)
        grads = jnp.concatenate([g_ref[:, c] for c in columns], axis=0)
        top8 = None
        for p in range(SPAN):
            rows = slice(p * ROWS, (p + 1) * ROWS)
            hide = bias[rows, :]
            s = dot_nt(kn[rows, :], normed) + jnp.concatenate([hide, hide], axis=1)
            scores[pair, rows, :] = s
            high = jnp.max(s.reshape(ROWS // 8, 8, 2 * ROWS), axis=0)
            top8 = high if top8 is None else jnp.maximum(top8, high)
        top = jnp.max(top8, axis=0, keepdims=True) * EXP2_SCALE
        total8 = jnp.zeros((8, 2 * ROWS), F32)
        for p in range(SPAN):
            rows = slice(p * ROWS, (p + 1) * ROWS)
            e = jnp.exp2(scores[pair, rows, :] * EXP2_SCALE - top)
            scores[pair, rows, :] = e
            total8 = total8 + fold(e)
            dprob[pair, rows, :] = dot_nt(win_ref[p, ROWS : 2 * ROWS, :], grads)
        inverse_total = 1.0 / jnp.sum(total8, axis=0, keepdims=True)
        delta8 = jnp.zeros((8, 2 * ROWS), F32)
        for p in range(SPAN):
            rows = slice(p * ROWS, (p + 1) * ROWS)
            rounded = (scores[pair, rows, :] * inverse_total).astype(BF16)
            probs_b[pair, rows, :] = rounded
            delta8 = delta8 + fold(rounded.astype(F32) * dprob[pair, rows, :])
        delta = jnp.sum(delta8, axis=0, keepdims=True)
        for p in range(SPAN):
            rows = slice(p * ROWS, (p + 1) * ROWS)
            prob = scores[pair, rows, :] * inverse_total
            dscore[pair, rows, :] = (prob * (dprob[pair, rows, :] - delta)).astype(BF16)
        dv[...] += dot_nn(probs_b[pair], grads)
        dk[...] += dot_nn(dscore[pair], normed)
        dq = dot_nn(knt[...], dscore[pair]).T * SCALE
        gain_rows = jnp.zeros((8, HEAD_SIZE), F32)
        for h in (0, 1):
            unit, inverse = units[h]
            part = dq[h * ROWS : (h + 1) * ROWS, :]
            qgrad_ref[:, columns[h]] = norm_backward(part, unit, inverse, qgain).astype(BF16)
            gain_rows = gain_rows + fold(part * unit)
        qsum[...] += gain_rows

    @pl.when(step == pl.num_programs(0) - 1)
    def _():
        ksum = jnp.zeros((8, HEAD_SIZE), F32)
        for p in range(SPAN):
            rows = slice(p * ROWS, (p + 1) * ROWS)
            unit, _ = unit_of(win_ref[p, :ROWS, :].astype(F32))
            part = dk[rows, :] * SCALE
            ksum = ksum + fold(part * unit)
            parts_ref[p, :ROWS, :] = part.astype(BF16)
            parts_ref[p, ROWS : 2 * ROWS, :] = dv[rows, :].astype(BF16)
        q_high, q_low = split(jnp.sum(qsum[...], axis=0, keepdims=True))
        k_high, k_low = split(jnp.sum(ksum, axis=0, keepdims=True))
        row = lax.broadcasted_iota(jnp.int32, (EXTRA, HEAD_SIZE), 0)
        extra = jnp.zeros((EXTRA, HEAD_SIZE), F32)
        for i, x in enumerate((q_high, q_low, k_high, k_low)):
            extra = jnp.where(row == i, x.astype(F32), extra)
        for p in range(SPAN):
            parts_ref[p, 2 * ROWS :, :] = extra.astype(BF16)


def attention(here, queries, gradient, window, segments, qgain, kgain):
    steps = HEADS // (2 * PAIRS)
    width = 2 * PAIRS * HEAD_SIZE
    whole = lambda shape: pl.BlockSpec(shape, lambda i: (0,) * len(shape))
    return pl.pallas_call(
        attention_kernel,
        grid=(steps,),
        in_specs=[
            pl.BlockSpec(memory_space=pltpu.SMEM),
            pl.BlockSpec((ROWS, width), lambda i: (0, i)),
            pl.BlockSpec((ROWS, width), lambda i: (0, i)),
            whole((SPAN, CHUNK, HEAD_SIZE)),
            whole((1, ROWS)),
            whole((1, HEAD_SIZE)),
            whole((1, HEAD_SIZE)),
        ],
        out_specs=[
            pl.BlockSpec((ROWS, width), lambda i: (0, i)),
            whole((SPAN, CHUNK, HEAD_SIZE)),
        ],
        out_shape=[
            jax.ShapeDtypeStruct((ROWS, HEADS * HEAD_SIZE), BF16),
            jax.ShapeDtypeStruct((SPAN, CHUNK, HEAD_SIZE), BF16),
        ],
        scratch_shapes=[
            pltpu.VMEM((TOKENS, HEAD_SIZE), BF16),
            pltpu.VMEM((HEAD_SIZE, TOKENS), BF16),
            pltpu.VMEM((TOKENS, ROWS), F32),
            pltpu.VMEM((PAIRS, TOKENS, 2 * ROWS), F32),
            pltpu.VMEM((PAIRS, TOKENS, 2 * ROWS), F32),
            pltpu.VMEM((PAIRS, TOKENS, 2 * ROWS), BF16),
            pltpu.VMEM((PAIRS, TOKENS, 2 * ROWS), BF16),
            pltpu.VMEM((TOKENS, HEAD_SIZE), F32),
            pltpu.VMEM((TOKENS, HEAD_SIZE), F32),
            pltpu.VMEM((8, HEAD_SIZE), F32),
        ],
        compiler_params=pltpu.CompilerParams(vmem_limit_bytes=40 * 2**20),
        name="attention_backward",
    )(here, queries, gradient, window, segments, qgain, kgain)


def combine_kernel(here_ref, parts_ref, own_ref, prev_ref, sums_ref):
    here = here_ref[0]
    for block in (0, 1):
        rows = slice(block * ROWS, (block + 1) * ROWS)
        own = jnp.zeros((ROWS, HEAD_SIZE), F32)
        prev = jnp.zeros((ROWS, HEAD_SIZE), F32)
        for p in range(SPAN):
            part = parts_ref[p, rows, :].astype(F32)
            is_own = p >= here
            own = own + jnp.where(is_own, part, 0.0)
            prev = prev + jnp.where(is_own, 0.0, part)
        own_ref[rows, :] = own
        prev_ref[rows, :] = prev.astype(BF16)
    extra = jnp.zeros((EXTRA, HEAD_SIZE), F32)
    for p in range(SPAN):
        extra = extra + parts_ref[p, 2 * ROWS :, :].astype(F32)
    qsum = extra[0:1, :] + extra[1:2, :]
    ksum = extra[2:3, :] + extra[3:4, :]
    both = jnp.concatenate([qsum, ksum], axis=0)
    sums_ref[...] = jnp.broadcast_to(both[None], sums_ref.shape)


def final_kernel(factor, own_ref, back_ref, key_ref, kgain_ref, sums_ref, kgrad_ref, vgrad_ref, gq_ref, gk_ref):
    unit, inverse = unit_of(key_ref[...].astype(F32))
    dk = own_ref[:ROWS, :] + back_ref[:ROWS, :].astype(F32)
    kgrad_ref[...] = norm_backward(dk, unit, inverse, kgain_ref[...]).astype(BF16)
    vgrad_ref[...] = (own_ref[ROWS:, :] + back_ref[ROWS:, :].astype(F32)).astype(BF16)
    sums = jnp.sum(sums_ref[...], axis=0) * factor
    gq_ref[...] = sums[0:1, :]
    gk_ref[...] = sums[1:2, :]


def per_device(queries, keys, value, gradient, segments, qgain, kgain):
    here = lax.axis_index(ROW)
    rest = lax.axis_size(REST)
    seq = lax.axis_size(SEQ)
    qgain, kgain = qgain.reshape(1, -1), kgain.reshape(1, -1)
    marks = jnp.broadcast_to(segments.astype(BF16)[None], (EXTRA, ROWS))
    own = jnp.concatenate([keys, value, marks], axis=0)
    previous = lax.ppermute(own, SEQ, [(i, (i + SPAN) % seq) for i in range(seq)])
    is_own = jnp.arange(SPAN) >= here
    outgoing = jnp.where(is_own[:, None, None], own[None], previous[None])
    window = lax.all_to_all(outgoing, ROW, 0, 0)
    place = here.astype(jnp.int32).reshape(1)
    qgrad, parts = attention(place, queries, gradient, window, segments.reshape(1, -1), qgain, kgain)
    returned = lax.all_to_all(parts, ROW, 0, 0)
    smem = pl.BlockSpec(memory_space=pltpu.SMEM)
    vmem = pl.BlockSpec(memory_space=pltpu.VMEM)
    mine, prev, sums = pl.pallas_call(
        combine_kernel,
        in_specs=[smem, vmem],
        out_specs=[vmem] * 3,
        out_shape=[
            jax.ShapeDtypeStruct((2 * ROWS, HEAD_SIZE), F32),
            jax.ShapeDtypeStruct((2 * ROWS, HEAD_SIZE), BF16),
            jax.ShapeDtypeStruct((rest, 2, HEAD_SIZE), F32),
        ],
        name="combine_partials",
    )(place, returned)
    back = lax.ppermute(prev, SEQ, [((i + SPAN) % seq, i) for i in range(seq)])
    sums = lax.all_to_all(sums, REST, 0, 0)
    factor = 1.0 / math.sqrt(ROWS * seq * HEADS * lax.axis_size("tp"))
    kgrad, vgrad, gq, gk = pl.pallas_call(
        lambda *refs: final_kernel(factor, *refs),
        in_specs=[vmem] * 5,
        out_specs=[vmem] * 4,
        out_shape=[
            jax.ShapeDtypeStruct((ROWS, HEAD_SIZE), BF16),
            jax.ShapeDtypeStruct((ROWS, HEAD_SIZE), BF16),
            jax.ShapeDtypeStruct((1, HEAD_SIZE), F32),
            jax.ShapeDtypeStruct((1, HEAD_SIZE), F32),
        ],
        name="finish_gradients",
    )(mine, back, keys, kgain, sums)
    return qgrad, kgrad, vgrad, gq.reshape(-1), gk.reshape(-1)


def solution(mesh):
    outer, ep, tp = mesh.devices.shape
    fine = Mesh(
        mesh.devices.reshape(2, outer // 4, 2, ep, tp), ("yl", "z", "core", "ep", "tp")
    )
    tokens = P(SEQ, "tp")
    return jax.shard_map(
        per_device,
        mesh=fine,
        in_specs=(tokens, tokens, tokens, tokens, P(SEQ), P(), P()),
        out_specs=(tokens, tokens, tokens, P(), P()),
        check_vma=False,
    )
```

```python
import math

import jax
import jax.numpy as jnp
from jax import lax
from jax.experimental import pallas as pl
from jax.experimental.pallas import tpu as pltpu
from jax.sharding import Mesh
from jax.sharding import PartitionSpec as P

HEAD_SIZE = 128
ROWS = 128
SPAN = 8
HEADS = 16
WIDE = 256
GROUPS = HEADS * ROWS // WIDE
TOKENS = SPAN * ROWS
EXTRA = 16
CHUNK = 2 * ROWS + EXTRA
EPS = 1e-06
NEG = -1e30
SCALE = 1.0 / math.sqrt(HEAD_SIZE)
EXP2_SCALE = SCALE * math.log2(math.e)

SEQ = ("yl", "z", "core", "ep")
ROW = ("core", "ep")
REST = ("yl", "z", "tp")
F32 = jnp.float32
BF16 = jnp.bfloat16


def dot_nt(a, b):
    return lax.dot_general(a, b, (((1,), (1,)), ((), ())), preferred_element_type=F32)


def dot_nn(a, b):
    return lax.dot_general(a, b, (((1,), (0,)), ((), ())), preferred_element_type=F32)


def unit_of(raw):
    inverse = lax.rsqrt(jnp.mean(raw * raw, axis=-1, keepdims=True) + EPS)
    return raw * inverse, inverse


def norm_backward(grad, unit, inverse, gain):
    scaled = grad * gain
    inner = jnp.mean(scaled * unit, axis=-1, keepdims=True)
    return inverse * (scaled - unit * inner)


def fold(x):
    return jnp.sum(x.reshape(x.shape[0] // 8, 8, x.shape[1]), axis=0)


def split(x):
    high = x.astype(BF16)
    return high, (x - high.astype(F32)).astype(BF16)


def interleave(*work):
    work = list(work)
    while work:
        for steps in list(work):
            if next(steps, steps) is steps:
                work.remove(steps)


def prepare_kernel(q_ref, g_ref, qgain_ref, kgain_ref, qn_ref, gh_ref, gains_ref):
    qgain = qgain_ref[...]
    for h in range(HEADS):
        columns = slice(h * HEAD_SIZE, (h + 1) * HEAD_SIZE)
        rows = slice(h * ROWS, (h + 1) * ROWS)
        unit, _ = unit_of(q_ref[:, columns].astype(F32))
        qn_ref[rows, :] = (unit * qgain).astype(BF16)
        gh_ref[rows, :] = g_ref[:, columns]
    row = lax.broadcasted_iota(jnp.int32, (8, HEAD_SIZE), 0)
    gains_ref[...] = jnp.where(row == 0, qgain, kgain_ref[...])


def attention_kernel(
    here_ref, qn_ref, g_ref, win_ref, own_ref, gains_ref,
    parts_ref, dqt_ref,
    kn, knt, vals, bias, scores, dprob, probs_b, dscore, dk, dv,
):
    qgain = gains_ref[0:1, :]
    kgain = gains_ref[1:2, :]
    here = here_ref[0]
    key_row = lax.broadcasted_iota(jnp.int32, (ROWS, ROWS), 0)
    query_col = lax.broadcasted_iota(jnp.int32, (ROWS, ROWS), 1)
    seg_q = jnp.broadcast_to(own_ref[2 * ROWS :, :].astype(F32)[0:1, :], (ROWS, ROWS))
    for p in range(SPAN):
        rows = slice(p * ROWS, (p + 1) * ROWS)
        unit, _ = unit_of(win_ref[p, :ROWS, :].astype(F32))
        normed = unit * kgain
        kn[rows, :] = normed.astype(BF16)
        knt[:, rows] = normed.T.astype(BF16)
        vals[rows, :] = win_ref[p, ROWS : 2 * ROWS, :]
        marks = win_ref[p, 2 * ROWS : 2 * ROWS + EXTRA, :].astype(F32)[0:1, :]
        seg_k = jnp.broadcast_to(marks, (ROWS, ROWS)).T
        late = jnp.where(here == p, 1, 0) * key_row > query_col
        hidden = jnp.logical_or(seg_k != seg_q, late)
        bias[rows, :] = jnp.where(hidden, NEG, 0.0)

    blocks = [slice(p * ROWS, (p + 1) * ROWS) for p in range(SPAN)]
    totals = [None] * GROUPS

    def softmax_steps(n):
        slot, cols = n % 2, slice(n * WIDE, (n + 1) * WIDE)
        top8 = jnp.full((8, WIDE), 2 * NEG, F32)
        for rows in blocks:
            hide = jnp.concatenate([bias[rows, :]] * (WIDE // ROWS), axis=1)
            s = dot_nt(kn[rows, :], qn_ref[cols, :]) + hide
            scores[slot, rows, :] = s
            top8 = jnp.maximum(top8, jnp.max(s.reshape(ROWS // 8, 8, WIDE), axis=0))
            yield
        top = jnp.max(top8, axis=0, keepdims=True) * EXP2_SCALE
        total8 = jnp.zeros((8, WIDE), F32)
        for rows in blocks:
            e = jnp.exp2(scores[slot, rows, :] * EXP2_SCALE - top)
            scores[slot, rows, :] = e
            total8 = total8 + fold(e)
            yield
        totals[n] = jnp.sum(total8, axis=0, keepdims=True)

    def gradient_steps(n):
        slot, cols = n % 2, slice(n * WIDE, (n + 1) * WIDE)
        inverse_total = 1.0 / totals[n]
        delta8 = jnp.zeros((8, WIDE), F32)
        for rows in blocks:
            rounded = (scores[slot, rows, :] * inverse_total).astype(BF16)
            probs_b[slot, rows, :] = rounded
            d = dot_nt(vals[rows, :], g_ref[cols, :])
            dprob[rows, :] = d
            delta8 = delta8 + fold(rounded.astype(F32) * d)
            yield
        delta = jnp.sum(delta8, axis=0, keepdims=True)
        for rows in blocks:
            prob = scores[slot, rows, :] * inverse_total
            dscore[slot, rows, :] = (prob * (dprob[rows, :] - delta)).astype(BF16)
            yield

    def sum_steps(n):
        slot, cols = n % 2, slice(n * WIDE, (n + 1) * WIDE)
        for rows in (slice(0, TOKENS // 2), slice(TOKENS // 2, TOKENS)):
            v = dot_nn(probs_b[slot, rows, :], g_ref[cols, :])
            dv[rows, :] = v if n == 0 else dv[rows, :] + v
            yield
        for rows in (slice(0, TOKENS // 2), slice(TOKENS // 2, TOKENS)):
            k = dot_nn(dscore[slot, rows, :], qn_ref[cols, :])
            dk[rows, :] = k if n == 0 else dk[rows, :] + k
            yield
        dqt_ref[:, cols] = dot_nn(knt[...], dscore[slot]) * SCALE
        yield

    interleave(softmax_steps(0))
    for n in range(GROUPS):
        work = [gradient_steps(n)]
        if n + 1 < GROUPS:
            work.append(softmax_steps(n + 1))
        if n:
            work.append(sum_steps(n - 1))
        interleave(*work)
    interleave(sum_steps(GROUPS - 1))

    ksum = jnp.zeros((8, HEAD_SIZE), F32)
    qsum = jnp.zeros((8, HEAD_SIZE), F32)
    for p, rows in enumerate(blocks):
        unit, _ = unit_of(win_ref[p, :ROWS, :].astype(F32))
        part = dk[rows, :] * SCALE
        ksum = ksum + fold(part * unit)
        qsum = qsum + fold(part * kn[rows, :].astype(F32))
        parts_ref[p, :ROWS, :] = part.astype(BF16)
        parts_ref[p, ROWS : 2 * ROWS, :] = dv[rows, :].astype(BF16)
    q_high, q_low = split(jnp.sum(qsum, axis=0, keepdims=True) / qgain)
    k_high, k_low = split(jnp.sum(ksum, axis=0, keepdims=True))
    row = lax.broadcasted_iota(jnp.int32, (EXTRA, HEAD_SIZE), 0)
    extra = jnp.zeros((EXTRA, HEAD_SIZE), F32)
    for i, x in enumerate((q_high, q_low, k_high, k_low)):
        extra = jnp.where(row == i, x.astype(F32), extra)
    for p in range(SPAN):
        parts_ref[p, 2 * ROWS :, :] = extra.astype(BF16)


def finish_query_kernel(dqt_ref, q_ref, qgain_ref, qgrad_ref):
    qgain = qgain_ref[...]
    for h in range(HEADS):
        columns = slice(h * HEAD_SIZE, (h + 1) * HEAD_SIZE)
        unit, inverse = unit_of(q_ref[:, columns].astype(F32))
        dq = dqt_ref[:, h * ROWS : (h + 1) * ROWS].T
        qgrad_ref[:, columns] = norm_backward(dq, unit, inverse, qgain).astype(BF16)


def combine_kernel(here_ref, parts_ref, own_ref, prev_ref, sums_ref):
    here = here_ref[0]
    for block in (0, 1):
        rows = slice(block * ROWS, (block + 1) * ROWS)
        own = jnp.zeros((ROWS, HEAD_SIZE), F32)
        prev = jnp.zeros((ROWS, HEAD_SIZE), F32)
        for p in range(SPAN):
            part = parts_ref[p, rows, :].astype(F32)
            is_own = p >= here
            own = own + jnp.where(is_own, part, 0.0)
            prev = prev + jnp.where(is_own, 0.0, part)
        own_ref[rows, :] = own
        prev_ref[rows, :] = prev.astype(BF16)
    extra = jnp.zeros((EXTRA, HEAD_SIZE), F32)
    for p in range(SPAN):
        extra = extra + parts_ref[p, 2 * ROWS :, :].astype(F32)
    qsum = extra[0:1, :] + extra[1:2, :]
    ksum = extra[2:3, :] + extra[3:4, :]
    both = jnp.concatenate([qsum, ksum], axis=0)
    sums_ref[...] = jnp.broadcast_to(both[None], sums_ref.shape)


def finish_key_kernel(own_ref, back_ref, key_ref, kgain_ref, kgrad_ref, vgrad_ref):
    unit, inverse = unit_of(key_ref[...].astype(F32))
    dk = own_ref[:ROWS, :] + back_ref[:ROWS, :].astype(F32)
    kgrad_ref[...] = norm_backward(dk, unit, inverse, kgain_ref[...]).astype(BF16)
    vgrad_ref[...] = (own_ref[ROWS:, :] + back_ref[ROWS:, :].astype(F32)).astype(BF16)


VMEM = pl.BlockSpec(memory_space=pltpu.VMEM)
SMEM = pl.BlockSpec(memory_space=pltpu.SMEM)


def call(kernel, name, operands, outs, mib, scratch=(), flops=0, data=0, scalar=False):
    return pl.pallas_call(
        kernel,
        in_specs=([SMEM] if scalar else []) + [VMEM] * (len(operands) - scalar),
        out_specs=[VMEM] * len(outs),
        out_shape=[jax.ShapeDtypeStruct(*out) for out in outs],
        scratch_shapes=list(scratch),
        compiler_params=pltpu.CompilerParams(vmem_limit_bytes=mib * 2**20),
        cost_estimate=pl.CostEstimate(flops=flops, bytes_accessed=data, transcendentals=0),
        name=name,
    )(*operands)


def per_device(queries, keys, value, gradient, segments, qgain, kgain):
    here = lax.axis_index(ROW)
    rest = lax.axis_size(REST)
    seq = lax.axis_size(SEQ)
    heads = HEADS * ROWS
    qgain, kgain = qgain.reshape(1, -1), kgain.reshape(1, -1)
    marks = jnp.broadcast_to(segments.astype(BF16)[None], (EXTRA, ROWS))
    own = jnp.concatenate([keys, value, marks], axis=0)
    previous = lax.ppermute(own, SEQ, [(i, (i + SPAN) % seq) for i in range(seq)])
    normed, gradient, gains = call(
        prepare_kernel, "prepare_queries", (queries, gradient, qgain, kgain),
        [((heads, HEAD_SIZE), BF16), ((heads, HEAD_SIZE), BF16), ((8, HEAD_SIZE), F32)],
        4, flops=10**9, data=2 * 10**6,
    )
    previous, normed, gradient, gains = lax.optimization_barrier((previous, normed, gradient, gains))
    is_own = jnp.arange(SPAN) >= here
    outgoing = jnp.where(is_own[:, None, None], own[None], previous[None])
    window = lax.all_to_all(outgoing, ROW, 0, 0)
    place = here.astype(jnp.int32).reshape(1)
    parts, dqt = call(
        attention_kernel, "attention_backward", (place, normed, gradient, window, own, gains),
        [((SPAN, CHUNK, HEAD_SIZE), BF16), ((HEAD_SIZE, heads), F32)],
        16,
        scratch=[
            pltpu.VMEM((TOKENS, HEAD_SIZE), BF16),
            pltpu.VMEM((HEAD_SIZE, TOKENS), BF16),
            pltpu.VMEM((TOKENS, HEAD_SIZE), BF16),
            pltpu.VMEM((TOKENS, ROWS), F32),
            pltpu.VMEM((2, TOKENS, WIDE), F32),
            pltpu.VMEM((TOKENS, WIDE), F32),
            pltpu.VMEM((2, TOKENS, WIDE), BF16),
            pltpu.VMEM((2, TOKENS, WIDE), BF16),
            pltpu.VMEM((TOKENS, HEAD_SIZE), F32),
            pltpu.VMEM((TOKENS, HEAD_SIZE), F32),
        ],
        flops=4 * 10**9, data=10**7, scalar=True,
    )
    returned = lax.all_to_all(parts, ROW, 0, 0)
    (qgrad,) = call(
        finish_query_kernel, "finish_queries", (dqt, queries, qgain),
        [((ROWS, heads), BF16)], 4, flops=10**9, data=2 * 10**6,
    )
    mine, prev, sums = call(
        combine_kernel, "combine_partials", (place, returned),
        [((2 * ROWS, HEAD_SIZE), F32), ((2 * ROWS, HEAD_SIZE), BF16), ((rest, 2, HEAD_SIZE), F32)],
        4, flops=10**8, data=10**6, scalar=True,
    )
    back = lax.ppermute(prev, SEQ, [((i + SPAN) % seq, i) for i in range(seq)])
    sums = lax.all_to_all(sums, REST, 0, 0)
    kgrad, vgrad = call(
        finish_key_kernel, "finish_keys", (mine, back, keys, kgain),
        [((ROWS, HEAD_SIZE), BF16), ((ROWS, HEAD_SIZE), BF16)], 4, flops=10**8, data=10**6,
    )
    factor = 1.0 / math.sqrt(ROWS * seq * HEADS * lax.axis_size("tp"))
    sums = jnp.sum(sums, axis=0) * factor
    return qgrad, kgrad, vgrad, sums[0], sums[1]


def solution(mesh):
    outer, ep, tp = mesh.devices.shape
    fine = Mesh(
        mesh.devices.reshape(2, outer // 4, 2, ep, tp), ("yl", "z", "core", "ep", "tp")
    )
    tokens = P(SEQ, "tp")
    return jax.shard_map(
        per_device,
        mesh=fine,
        in_specs=(tokens, tokens, tokens, tokens, P(SEQ), P(), P()),
        out_specs=(tokens, tokens, tokens, P(), P()),
        check_vma=False,
    )
```

```python
import functools
import math

import jax
import jax.numpy as jnp
from jax import lax
from jax.experimental import pallas as pl
from jax.experimental.pallas import tpu as pltpu
from jax.sharding import Mesh
from jax.sharding import PartitionSpec as P

HEAD_SIZE = 128
ROWS = 128
SPAN = 8
HEADS = 16
WIDE = 256
GROUPS = HEADS * ROWS // WIDE
TOKENS = SPAN * ROWS
EXTRA = 16
CHUNK = 2 * ROWS + EXTRA
EPS = 1e-06
NEG = -1e30
SCALE = 1.0 / math.sqrt(HEAD_SIZE)
EXP2_SCALE = SCALE * math.log2(math.e)

SEQ = ("yl", "z", "core", "ep")
ROW = ("core", "ep")
REST = ("yl", "z", "tp")
F32 = jnp.float32
BF16 = jnp.bfloat16


def dot_nt(a, b):
    return lax.dot_general(a, b, (((1,), (1,)), ((), ())), preferred_element_type=F32)


def dot_nn(a, b):
    return lax.dot_general(a, b, (((1,), (0,)), ((), ())), preferred_element_type=F32)


def unit_of(raw):
    inverse = lax.rsqrt(jnp.mean(raw * raw, axis=-1, keepdims=True) + EPS)
    return raw * inverse, inverse


def norm_backward(grad, unit, inverse, gain):
    scaled = grad * gain
    inner = jnp.mean(scaled * unit, axis=-1, keepdims=True)
    return inverse * (scaled - unit * inner)


def fold(x):
    return jnp.sum(x.reshape(x.shape[0] // 8, 8, x.shape[1]), axis=0)


def split(x):
    high = x.astype(BF16)
    return high, (x - high.astype(F32)).astype(BF16)


def interleave(*work):
    work = list(work)
    while work:
        for steps in list(work):
            if next(steps, steps) is steps:
                work.remove(steps)


def prepare_kernel(q_ref, g_ref, qgain_ref, kgain_ref, qn_ref, gh_ref, gains_ref):
    qgain = qgain_ref[...]
    for h in range(HEADS):
        columns = slice(h * HEAD_SIZE, (h + 1) * HEAD_SIZE)
        rows = slice(h * ROWS, (h + 1) * ROWS)
        unit, _ = unit_of(q_ref[:, columns].astype(F32))
        qn_ref[rows, :] = (unit * qgain).astype(BF16)
        gh_ref[rows, :] = g_ref[:, columns]
    row = lax.broadcasted_iota(jnp.int32, (8, HEAD_SIZE), 0)
    gains_ref[...] = jnp.where(row == 0, qgain, kgain_ref[...])


def attention_kernel(
    here_ref, qn_ref, g_ref, win_ref, own_ref, gains_ref,
    parts_ref, dqt_ref,
    kn, knt, vals, bias, scores, dprob, probs_b, dscore, dk, dv,
):
    qgain = gains_ref[0:1, :]
    kgain = gains_ref[1:2, :]
    here = here_ref[0]
    key_row = lax.broadcasted_iota(jnp.int32, (ROWS, ROWS), 0)
    query_col = lax.broadcasted_iota(jnp.int32, (ROWS, ROWS), 1)
    seg_q = jnp.broadcast_to(own_ref[2 * ROWS :, :].astype(F32)[0:1, :], (ROWS, ROWS))
    last = 2 * ROWS + EXTRA
    marks = [win_ref[p, 2 * ROWS : last, :].astype(F32)[0:1, :] for p in range(SPAN)]
    marks = jnp.concatenate(marks, axis=0).T
    for p in range(SPAN):
        rows = slice(p * ROWS, (p + 1) * ROWS)
        unit, _ = unit_of(win_ref[p, :ROWS, :].astype(F32))
        normed = (unit * kgain).astype(BF16)
        kn[rows, :] = normed
        knt[:, rows] = normed.T
        vals[rows, :] = win_ref[p, ROWS : 2 * ROWS, :]
        late = jnp.where(here == p, 1, 0) * key_row > query_col
        hidden = jnp.logical_or(marks[:, p : p + 1] != seg_q, late)
        bias[rows, :] = jnp.where(hidden, NEG, 0.0)

    blocks = [slice(p * ROWS, (p + 1) * ROWS) for p in range(SPAN)]
    totals = [None] * GROUPS

    def softmax_steps(n):
        slot, cols = n % 2, slice(n * WIDE, (n + 1) * WIDE)
        top8 = jnp.full((8, WIDE), 2 * NEG, F32)
        for rows in blocks:
            hide = jnp.concatenate([bias[rows, :]] * (WIDE // ROWS), axis=1)
            s = dot_nt(kn[rows, :], qn_ref[cols, :]) + hide
            s = s * EXP2_SCALE
            scores[slot, rows, :] = s
            top8 = jnp.maximum(top8, jnp.max(s.reshape(ROWS // 8, 8, WIDE), axis=0))
            yield
        top = jnp.max(top8, axis=0, keepdims=True)
        total8 = jnp.zeros((8, WIDE), F32)
        for rows in blocks:
            e = jnp.exp2(scores[slot, rows, :] - top)
            scores[slot, rows, :] = e
            total8 = total8 + fold(e)
            yield
        totals[n] = jnp.sum(total8, axis=0, keepdims=True)

    def gradient_steps(n):
        slot, cols = n % 2, slice(n * WIDE, (n + 1) * WIDE)
        inverse_total = 1.0 / totals[n]
        delta8 = jnp.zeros((8, WIDE), F32)
        for rows in blocks:
            prob = scores[slot, rows, :] * inverse_total
            scores[slot, rows, :] = prob
            rounded = prob.astype(BF16)
            probs_b[slot, rows, :] = rounded
            d = dot_nt(vals[rows, :], g_ref[cols, :])
            dprob[rows, :] = d
            delta8 = delta8 + fold(rounded.astype(F32) * d)
            yield
        delta = jnp.sum(delta8, axis=0, keepdims=True)
        for rows in blocks:
            prob = scores[slot, rows, :]
            dscore[slot, rows, :] = (prob * (dprob[rows, :] - delta)).astype(BF16)
            yield

    def sum_steps(n):
        slot, cols = n % 2, slice(n * WIDE, (n + 1) * WIDE)
        for rows in (slice(0, TOKENS // 2), slice(TOKENS // 2, TOKENS)):
            v = dot_nn(probs_b[slot, rows, :], g_ref[cols, :])
            dv[rows, :] = v if n == 0 else dv[rows, :] + v
            yield
        for rows in (slice(0, TOKENS // 2), slice(TOKENS // 2, TOKENS)):
            k = dot_nn(dscore[slot, rows, :], qn_ref[cols, :])
            dk[rows, :] = k if n == 0 else dk[rows, :] + k
            yield
        dqt_ref[:, cols] = dot_nn(knt[...], dscore[slot]) * SCALE
        yield

    interleave(softmax_steps(0))
    for n in range(GROUPS):
        work = [gradient_steps(n)]
        if n + 1 < GROUPS:
            work.append(softmax_steps(n + 1))
        if n:
            work.append(sum_steps(n - 1))
        interleave(*work)
    interleave(sum_steps(GROUPS - 1))

    ksum = jnp.zeros((8, HEAD_SIZE), F32)
    qsum = jnp.zeros((8, HEAD_SIZE), F32)
    for p, rows in enumerate(blocks):
        unit, _ = unit_of(win_ref[p, :ROWS, :].astype(F32))
        part = dk[rows, :] * SCALE
        ksum = ksum + fold(part * unit)
        qsum = qsum + fold(part * kn[rows, :].astype(F32))
        parts_ref[p, :ROWS, :] = part.astype(BF16)
        parts_ref[p, ROWS : 2 * ROWS, :] = dv[rows, :].astype(BF16)
    q_high, q_low = split(jnp.sum(qsum, axis=0, keepdims=True) / qgain)
    k_high, k_low = split(jnp.sum(ksum, axis=0, keepdims=True))
    row = lax.broadcasted_iota(jnp.int32, (EXTRA, HEAD_SIZE), 0)
    extra = jnp.zeros((EXTRA, HEAD_SIZE), F32)
    for i, x in enumerate((q_high, q_low, k_high, k_low)):
        extra = jnp.where(row == i, x.astype(F32), extra)
    for p in range(SPAN):
        parts_ref[p, 2 * ROWS :, :] = extra.astype(BF16)


def finish_query_kernel(dqt_ref, q_ref, qgain_ref, qgrad_ref):
    qgain = qgain_ref[...]
    for h in range(HEADS):
        columns = slice(h * HEAD_SIZE, (h + 1) * HEAD_SIZE)
        unit, inverse = unit_of(q_ref[:, columns].astype(F32))
        dq = dqt_ref[:, h * ROWS : (h + 1) * ROWS].T
        qgrad_ref[:, columns] = norm_backward(dq, unit, inverse, qgain).astype(BF16)


def combine_kernel(factor, here_ref, parts_ref, own_ref, prev_ref, sums_ref):
    here = here_ref[0]
    for block in (0, 1):
        rows = slice(block * ROWS, (block + 1) * ROWS)
        own = jnp.zeros((ROWS, HEAD_SIZE), F32)
        prev = jnp.zeros((ROWS, HEAD_SIZE), F32)
        for p in range(SPAN):
            part = parts_ref[p, rows, :].astype(F32)
            is_own = p >= here
            own = own + jnp.where(is_own, part, 0.0)
            prev = prev + jnp.where(is_own, 0.0, part)
        own_ref[rows, :] = own
        prev_ref[rows, :] = prev.astype(BF16)
    extra = jnp.zeros((EXTRA, HEAD_SIZE), F32)
    for p in range(SPAN):
        extra = extra + parts_ref[p, 2 * ROWS :, :].astype(F32)
    qsum = extra[0:1, :] + extra[1:2, :]
    ksum = extra[2:3, :] + extra[3:4, :]
    both = jnp.concatenate([qsum, ksum], axis=0) * factor
    sums_ref[...] = jnp.broadcast_to(both[None], sums_ref.shape)


def finish_key_kernel(own_ref, back_ref, key_ref, kgain_ref, kgrad_ref, vgrad_ref):
    unit, inverse = unit_of(key_ref[...].astype(F32))
    dk = own_ref[:ROWS, :] + back_ref[:ROWS, :].astype(F32)
    kgrad_ref[...] = norm_backward(dk, unit, inverse, kgain_ref[...]).astype(BF16)
    vgrad_ref[...] = (own_ref[ROWS:, :] + back_ref[ROWS:, :].astype(F32)).astype(BF16)


VMEM = pl.BlockSpec(memory_space=pltpu.VMEM)
SMEM = pl.BlockSpec(memory_space=pltpu.SMEM)


def call(kernel, name, operands, outs, mib, scratch=(), flops=0, data=0, scalar=False):
    return pl.pallas_call(
        kernel,
        in_specs=[SMEM] * scalar + [VMEM] * (len(operands) - scalar),
        out_specs=[VMEM] * len(outs),
        out_shape=[jax.ShapeDtypeStruct(*out) for out in outs],
        scratch_shapes=list(scratch),
        compiler_params=pltpu.CompilerParams(vmem_limit_bytes=mib * 2**20),
        cost_estimate=pl.CostEstimate(flops=flops, bytes_accessed=data, transcendentals=0),
        name=name,
    )(*operands)


def attention(*operands):
    heads = HEADS * ROWS
    return call(
        attention_kernel, "attention_backward", operands,
        [((SPAN, CHUNK, HEAD_SIZE), BF16), ((HEAD_SIZE, heads), F32)],
        16,
        scratch=[
            pltpu.VMEM((TOKENS, HEAD_SIZE), BF16),
            pltpu.VMEM((HEAD_SIZE, TOKENS), BF16),
            pltpu.VMEM((TOKENS, HEAD_SIZE), BF16),
            pltpu.VMEM((TOKENS, ROWS), F32),
            pltpu.VMEM((2, TOKENS, WIDE), F32),
            pltpu.VMEM((TOKENS, WIDE), F32),
            pltpu.VMEM((2, TOKENS, WIDE), BF16),
            pltpu.VMEM((2, TOKENS, WIDE), BF16),
            pltpu.VMEM((TOKENS, HEAD_SIZE), F32),
            pltpu.VMEM((TOKENS, HEAD_SIZE), F32),
        ],
        flops=4 * 10**9, data=10**7, scalar=True,
    )


def per_device(queries, keys, value, gradient, segments, qgain, kgain):
    here = lax.axis_index(ROW)
    rest = lax.axis_size(REST)
    seq = lax.axis_size(SEQ)
    heads = HEADS * ROWS
    qgain, kgain = qgain.reshape(1, -1), kgain.reshape(1, -1)
    room = jnp.zeros((EXTRA, HEAD_SIZE), BF16)
    own = jnp.concatenate([keys, value, room], axis=0)
    own, segments = lax.optimization_barrier((own, segments))
    own = own.at[2 * ROWS :].set(jnp.broadcast_to(segments.astype(BF16)[None], (EXTRA, ROWS)))
    previous = lax.ppermute(own, SEQ, [(i, (i + SPAN) % seq) for i in range(seq)])
    normed, gradient, gains = call(
        prepare_kernel, "prepare_queries", (queries, gradient, qgain, kgain),
        [((heads, HEAD_SIZE), BF16), ((heads, HEAD_SIZE), BF16), ((8, HEAD_SIZE), F32)],
        4, flops=10**9, data=2 * 10**6,
    )
    previous, normed, gradient, gains = lax.optimization_barrier((previous, normed, gradient, gains))
    is_own = jnp.arange(SPAN) >= here
    outgoing = jnp.where(is_own[:, None, None], own[None], previous[None])
    window = lax.all_to_all(outgoing, ROW, 0, 0)
    place = here.astype(jnp.int32).reshape(1)
    parts, dqt = attention(place, normed, gradient, window, own, gains)
    returned = lax.all_to_all(parts, ROW, 0, 0)
    (qgrad,) = call(
        finish_query_kernel, "finish_queries", (dqt, queries, qgain),
        [((ROWS, heads), BF16)], 4, flops=10**9, data=2 * 10**6,
    )
    factor = 1.0 / math.sqrt(ROWS * seq * HEADS * lax.axis_size("tp"))
    mine, prev, sums = call(
        functools.partial(combine_kernel, factor), "combine_partials", (place, returned),
        [((2 * ROWS, HEAD_SIZE), F32), ((2 * ROWS, HEAD_SIZE), BF16), ((rest, 2, HEAD_SIZE), F32)],
        4, flops=10**8, data=10**6, scalar=True,
    )
    back = lax.ppermute(prev, SEQ, [((i + SPAN) % seq, i) for i in range(seq)])
    sums = lax.all_to_all(sums, REST, 0, 0)
    kgrad, vgrad = call(
        finish_key_kernel, "finish_keys", (mine, back, keys, kgain),
        [((ROWS, HEAD_SIZE), BF16), ((ROWS, HEAD_SIZE), BF16)], 4, flops=10**8, data=10**6,
    )
    sums = jnp.sum(sums, axis=0)
    return qgrad, kgrad, vgrad, sums[0], sums[1]


def solution(mesh):
    outer, ep, tp = mesh.devices.shape
    fine = Mesh(
        mesh.devices.reshape(2, outer // 4, 2, ep, tp), ("yl", "z", "core", "ep", "tp")
    )
    tokens = P(SEQ, "tp")
    return jax.shard_map(
        per_device,
        mesh=fine,
        in_specs=(tokens, tokens, tokens, tokens, P(SEQ), P(), P()),
        out_specs=(tokens, tokens, tokens, P(), P()),
        check_vma=False,
    )
```

```python
import functools
import math

import jax
import jax.numpy as jnp
from jax import lax
from jax.experimental import pallas as pl
from jax.experimental.pallas import tpu as pltpu
from jax.sharding import Mesh
from jax.sharding import PartitionSpec as P

HEAD_SIZE = 128
ROWS = 128
SPAN = 8
HEADS = 16
WIDE = 256
GROUPS = HEADS * ROWS // WIDE
TOKENS = SPAN * ROWS
EXTRA = 16
CHUNK = 2 * ROWS + EXTRA
EPS = 1e-06
NEG = -1e30
SCALE = 1.0 / math.sqrt(HEAD_SIZE)
EXP2_SCALE = SCALE * math.log2(math.e)

SEQ = ("yl", "z", "core", "ep")
ROW = ("core", "ep")
REST = ("yl", "z", "tp")
F32 = jnp.float32
BF16 = jnp.bfloat16


def dot_nt(a, b):
    return lax.dot_general(a, b, (((1,), (1,)), ((), ())), preferred_element_type=F32)


def dot_nn(a, b):
    return lax.dot_general(a, b, (((1,), (0,)), ((), ())), preferred_element_type=F32)


def unit_of(raw):
    inverse = lax.rsqrt(jnp.mean(raw * raw, axis=-1, keepdims=True) + EPS)
    return raw * inverse, inverse


def norm_backward(grad, unit, inverse, gain):
    scaled = grad * gain
    inner = jnp.mean(scaled * unit, axis=-1, keepdims=True)
    return inverse * (scaled - unit * inner)


def fold(x):
    return jnp.sum(x.reshape(x.shape[0] // 8, 8, x.shape[1]), axis=0)


def split(x):
    high = x.astype(BF16)
    return high, (x - high.astype(F32)).astype(BF16)


def interleave(*work):
    work = list(work)
    while work:
        for steps in list(work):
            if next(steps, steps) is steps:
                work.remove(steps)


def prepare_kernel(q_ref, g_ref, qgain_ref, kgain_ref, qn_ref, gh_ref, gains_ref):
    qgain = qgain_ref[...]
    for h in range(HEADS):
        columns = slice(h * HEAD_SIZE, (h + 1) * HEAD_SIZE)
        rows = slice(h * ROWS, (h + 1) * ROWS)
        unit, _ = unit_of(q_ref[:, columns].astype(F32))
        qn_ref[rows, :] = (unit * qgain).astype(BF16)
        gh_ref[rows, :] = g_ref[:, columns]
    row = lax.broadcasted_iota(jnp.int32, (8, HEAD_SIZE), 0)
    gains_ref[...] = jnp.where(row == 0, qgain, kgain_ref[...])


def attention_kernel(
    here_ref, qn_ref, g_ref, win_ref, own_ref, gains_ref,
    parts_ref, dqt_ref,
    kn, knt, vals, bias, scores, dprob, probs_b, dscore, dk, dv,
):
    qgain = gains_ref[0:1, :]
    kgain = gains_ref[1:2, :]
    here = here_ref[0]
    key_row = lax.broadcasted_iota(jnp.int32, (ROWS, ROWS), 0)
    query_col = lax.broadcasted_iota(jnp.int32, (ROWS, ROWS), 1)
    seg_q = jnp.broadcast_to(own_ref[2 * ROWS :, :].astype(F32)[0:1, :], (ROWS, ROWS))
    last = 2 * ROWS + EXTRA
    marks = [win_ref[p, 2 * ROWS : last, :].astype(F32)[0:1, :] for p in range(SPAN)]
    marks = jnp.concatenate(marks, axis=0).T
    for p in range(SPAN):
        rows = slice(p * ROWS, (p + 1) * ROWS)
        unit, _ = unit_of(win_ref[p, :ROWS, :].astype(F32))
        normed = (unit * kgain).astype(BF16)
        kn[rows, :] = normed
        knt[:, rows] = normed.T
        vals[rows, :] = win_ref[p, ROWS : 2 * ROWS, :]
        late = jnp.where(here == p, 1, 0) * key_row > query_col
        hidden = jnp.logical_or(marks[:, p : p + 1] != seg_q, late)
        bias[rows, :] = jnp.where(hidden, NEG, 0.0)

    blocks = [slice(p * ROWS, (p + 1) * ROWS) for p in range(SPAN)]
    totals = [None] * GROUPS

    def softmax_steps(n):
        slot, cols = n % 2, slice(n * WIDE, (n + 1) * WIDE)
        top8 = jnp.full((8, WIDE), 2 * NEG, F32)
        for rows in blocks:
            hide = jnp.concatenate([bias[rows, :]] * (WIDE // ROWS), axis=1)
            s = dot_nt(kn[rows, :], qn_ref[cols, :]) + hide
            s = s * EXP2_SCALE
            scores[slot, rows, :] = s
            top8 = jnp.maximum(top8, jnp.max(s.reshape(ROWS // 8, 8, WIDE), axis=0))
            yield
        top = jnp.max(top8, axis=0, keepdims=True)
        total8 = jnp.zeros((8, WIDE), F32)
        for rows in blocks:
            e = jnp.exp2(scores[slot, rows, :] - top)
            scores[slot, rows, :] = e
            total8 = total8 + fold(e)
            yield
        totals[n] = jnp.sum(total8, axis=0, keepdims=True)

    def gradient_steps(n):
        slot, cols = n % 2, slice(n * WIDE, (n + 1) * WIDE)
        inverse_total = 1.0 / totals[n]
        delta8 = jnp.zeros((8, WIDE), F32)
        for rows in blocks:
            prob = scores[slot, rows, :] * inverse_total
            scores[slot, rows, :] = prob
            rounded = prob.astype(BF16)
            probs_b[slot, rows, :] = rounded
            d = dot_nt(vals[rows, :], g_ref[cols, :])
            dprob[rows, :] = d
            delta8 = delta8 + fold(rounded.astype(F32) * d)
            yield
        delta = jnp.sum(delta8, axis=0, keepdims=True)
        values = value_steps(n)
        for rows in blocks:
            next(values, None)
            prob = scores[slot, rows, :]
            dscore[slot, rows, :] = (prob * (dprob[rows, :] - delta)).astype(BF16)
            yield

    def value_steps(n):
        slot, cols = n % 2, slice(n * WIDE, (n + 1) * WIDE)
        for rows in (slice(0, TOKENS // 2), slice(TOKENS // 2, TOKENS)):
            v = dot_nn(probs_b[slot, rows, :], g_ref[cols, :])
            dv[rows, :] = v if n == 0 else dv[rows, :] + v
            yield

    def sum_steps(n):
        slot, cols = n % 2, slice(n * WIDE, (n + 1) * WIDE)
        for rows in (slice(0, TOKENS // 2), slice(TOKENS // 2, TOKENS)):
            k = dot_nn(dscore[slot, rows, :], qn_ref[cols, :])
            dk[rows, :] = k if n == 0 else dk[rows, :] + k
            yield
        dqt_ref[:, cols] = dot_nn(knt[...], dscore[slot]) * SCALE
        yield

    interleave(softmax_steps(0))
    for n in range(GROUPS):
        work = [gradient_steps(n)]
        if n + 1 < GROUPS:
            work.append(softmax_steps(n + 1))
        if n:
            work.append(sum_steps(n - 1))
        interleave(*work)
    interleave(sum_steps(GROUPS - 1))

    ksum = jnp.zeros((8, HEAD_SIZE), F32)
    qsum = jnp.zeros((8, HEAD_SIZE), F32)
    for p, rows in enumerate(blocks):
        unit, _ = unit_of(win_ref[p, :ROWS, :].astype(F32))
        part = dk[rows, :] * SCALE
        ksum = ksum + fold(part * unit)
        qsum = qsum + fold(part * kn[rows, :].astype(F32))
        parts_ref[p, :ROWS, :] = part.astype(BF16)
        parts_ref[p, ROWS : 2 * ROWS, :] = dv[rows, :].astype(BF16)
    q_high, q_low = split(jnp.sum(qsum, axis=0, keepdims=True) / qgain)
    k_high, k_low = split(jnp.sum(ksum, axis=0, keepdims=True))
    row = lax.broadcasted_iota(jnp.int32, (EXTRA, HEAD_SIZE), 0)
    extra = jnp.zeros((EXTRA, HEAD_SIZE), F32)
    for i, x in enumerate((q_high, q_low, k_high, k_low)):
        extra = jnp.where(row == i, x.astype(F32), extra)
    for p in range(SPAN):
        parts_ref[p, 2 * ROWS :, :] = extra.astype(BF16)


def finish_query_kernel(dqt_ref, q_ref, qgain_ref, qgrad_ref):
    qgain = qgain_ref[...]
    for h in range(HEADS):
        columns = slice(h * HEAD_SIZE, (h + 1) * HEAD_SIZE)
        unit, inverse = unit_of(q_ref[:, columns].astype(F32))
        dq = dqt_ref[:, h * ROWS : (h + 1) * ROWS].T
        qgrad_ref[:, columns] = norm_backward(dq, unit, inverse, qgain).astype(BF16)


def combine_kernel(here_ref, parts_ref, own_ref, prev_ref):
    here = here_ref[0]
    for block in (0, 1):
        rows = slice(block * ROWS, (block + 1) * ROWS)
        own = jnp.zeros((ROWS, HEAD_SIZE), F32)
        prev = jnp.zeros((ROWS, HEAD_SIZE), F32)
        for p in range(SPAN):
            part = parts_ref[p, rows, :].astype(F32)
            is_own = p >= here
            own = own + jnp.where(is_own, part, 0.0)
            prev = prev + jnp.where(is_own, 0.0, part)
        own_ref[rows, :] = own
        prev_ref[rows, :] = prev.astype(BF16)


def combine_sums_kernel(factor, parts_ref, sums_ref):
    extra = jnp.zeros((EXTRA, HEAD_SIZE), F32)
    for p in range(SPAN):
        extra = extra + parts_ref[p, 2 * ROWS :, :].astype(F32)
    qsum = extra[0:1, :] + extra[1:2, :]
    ksum = extra[2:3, :] + extra[3:4, :]
    both = jnp.concatenate([qsum, ksum], axis=0) * factor
    sums_ref[...] = jnp.broadcast_to(both[None], sums_ref.shape)


def finish_key_kernel(own_ref, back_ref, key_ref, kgain_ref, kgrad_ref, vgrad_ref):
    unit, inverse = unit_of(key_ref[...].astype(F32))
    dk = own_ref[:ROWS, :] + back_ref[:ROWS, :].astype(F32)
    kgrad_ref[...] = norm_backward(dk, unit, inverse, kgain_ref[...]).astype(BF16)
    vgrad_ref[...] = (own_ref[ROWS:, :] + back_ref[ROWS:, :].astype(F32)).astype(BF16)


VMEM = pl.BlockSpec(memory_space=pltpu.VMEM)
SMEM = pl.BlockSpec(memory_space=pltpu.SMEM)


def call(kernel, name, operands, outs, mib, scratch=(), flops=0, data=0, scalar=False):
    return pl.pallas_call(
        kernel,
        in_specs=[SMEM] * scalar + [VMEM] * (len(operands) - scalar),
        out_specs=[VMEM] * len(outs),
        out_shape=[jax.ShapeDtypeStruct(*out) for out in outs],
        scratch_shapes=list(scratch),
        compiler_params=pltpu.CompilerParams(vmem_limit_bytes=mib * 2**20),
        cost_estimate=pl.CostEstimate(flops=flops, bytes_accessed=data, transcendentals=0),
        name=name,
    )(*operands)


def attention(*operands):
    heads = HEADS * ROWS
    return call(
        attention_kernel, "attention_backward", operands,
        [((SPAN, CHUNK, HEAD_SIZE), BF16), ((HEAD_SIZE, heads), F32)],
        16,
        scratch=[
            pltpu.VMEM((TOKENS, HEAD_SIZE), BF16),
            pltpu.VMEM((HEAD_SIZE, TOKENS), BF16),
            pltpu.VMEM((TOKENS, HEAD_SIZE), BF16),
            pltpu.VMEM((TOKENS, ROWS), F32),
            pltpu.VMEM((2, TOKENS, WIDE), F32),
            pltpu.VMEM((TOKENS, WIDE), F32),
            pltpu.VMEM((2, TOKENS, WIDE), BF16),
            pltpu.VMEM((2, TOKENS, WIDE), BF16),
            pltpu.VMEM((TOKENS, HEAD_SIZE), F32),
            pltpu.VMEM((TOKENS, HEAD_SIZE), F32),
        ],
        flops=4 * 10**9, data=10**7, scalar=True,
    )


def per_device(queries, keys, value, gradient, segments, qgain, kgain):
    here = lax.axis_index(ROW)
    rest = lax.axis_size(REST)
    seq = lax.axis_size(SEQ)
    heads = HEADS * ROWS
    qgain, kgain = qgain.reshape(1, -1), kgain.reshape(1, -1)
    room = jnp.zeros((EXTRA, HEAD_SIZE), BF16)
    own = jnp.concatenate([keys, value, room], axis=0)
    own, segments = lax.optimization_barrier((own, segments))
    own = own.at[2 * ROWS :].set(jnp.broadcast_to(segments.astype(BF16)[None], (EXTRA, ROWS)))
    previous = lax.ppermute(own, SEQ, [(i, (i + SPAN) % seq) for i in range(seq)])
    normed, gradient, gains = call(
        prepare_kernel, "prepare_queries", (queries, gradient, qgain, kgain),
        [((heads, HEAD_SIZE), BF16), ((heads, HEAD_SIZE), BF16), ((8, HEAD_SIZE), F32)],
        4, flops=10**9, data=2 * 10**6,
    )
    previous, normed, gradient, gains = lax.optimization_barrier((previous, normed, gradient, gains))
    is_own = jnp.arange(SPAN) >= here
    outgoing = jnp.where(is_own[:, None, None], own[None], previous[None])
    window = lax.all_to_all(outgoing, ROW, 0, 0)
    place = here.astype(jnp.int32).reshape(1)
    parts, dqt = attention(place, normed, gradient, window, own, gains)
    returned = lax.all_to_all(parts, ROW, 0, 0)
    (qgrad,) = call(
        finish_query_kernel, "finish_queries", (dqt, queries, qgain),
        [((ROWS, heads), BF16)], 4, flops=10**9, data=2 * 10**6,
    )
    factor = 1.0 / math.sqrt(ROWS * seq * HEADS * lax.axis_size("tp"))
    (sums,) = call(
        functools.partial(combine_sums_kernel, factor), "combine_sums", (returned,),
        [((rest, 2, HEAD_SIZE), F32)], 4, data=10**5,
    )
    mine, prev = call(
        combine_kernel, "combine_partials", (place, returned),
        [((2 * ROWS, HEAD_SIZE), F32), ((2 * ROWS, HEAD_SIZE), BF16)],
        4, flops=10**8, data=10**6, scalar=True,
    )
    back = lax.ppermute(prev, SEQ, [((i + SPAN) % seq, i) for i in range(seq)])
    sums = lax.all_to_all(sums, REST, 0, 0)
    kgrad, vgrad = call(
        finish_key_kernel, "finish_keys", (mine, back, keys, kgain),
        [((ROWS, HEAD_SIZE), BF16), ((ROWS, HEAD_SIZE), BF16)], 4, flops=10**8, data=10**6,
    )
    sums = jnp.sum(sums, axis=0)
    return qgrad, kgrad, vgrad, sums[0], sums[1]


def solution(mesh):
    outer, ep, tp = mesh.devices.shape
    fine = Mesh(
        mesh.devices.reshape(2, outer // 4, 2, ep, tp), ("yl", "z", "core", "ep", "tp")
    )
    tokens = P(SEQ, "tp")
    return jax.shard_map(
        per_device,
        mesh=fine,
        in_specs=(tokens, tokens, tokens, tokens, P(SEQ), P(), P()),
        out_specs=(tokens, tokens, tokens, P(), P()),
        check_vma=False,
    )
```

```python
import math

import jax
import jax.numpy as jnp
from jax import lax
from jax.experimental import pallas as pl
from jax.experimental.pallas import tpu as pltpu
from jax.sharding import Mesh
from jax.sharding import PartitionSpec as P

HEAD_SIZE = 128
ROWS = 128
SPAN = 8
HEADS = 16
WIDE = 256
GROUPS = HEADS * ROWS // WIDE
TOKENS = SPAN * ROWS
EXTRA = 16
CHUNK = 2 * ROWS + EXTRA
EPS = 1e-06
NEG = -1e30
SCALE = 1.0 / math.sqrt(HEAD_SIZE)
EXP2_SCALE = SCALE * math.log2(math.e)

SEQ = ("yl", "z", "core", "ep")
ROW = ("core", "ep")
REST = ("yl", "z", "tp")
F32 = jnp.float32
BF16 = jnp.bfloat16


def dot_nt(a, b):
    return lax.dot_general(a, b, (((1,), (1,)), ((), ())), preferred_element_type=F32)


def dot_nn(a, b):
    return lax.dot_general(a, b, (((1,), (0,)), ((), ())), preferred_element_type=F32)


def unit_of(raw):
    inverse = lax.rsqrt(jnp.mean(raw * raw, axis=-1, keepdims=True) + EPS)
    return raw * inverse, inverse


def norm_backward(grad, unit, inverse, gain):
    scaled = grad * gain
    inner = jnp.mean(scaled * unit, axis=-1, keepdims=True)
    return inverse * (scaled - unit * inner)


def fold(x):
    return jnp.sum(x.reshape(x.shape[0] // 8, 8, x.shape[1]), axis=0)


def split(x):
    high = x.astype(BF16)
    return high, (x - high.astype(F32)).astype(BF16)


def interleave(*work):
    work = list(work)
    while work:
        for steps in list(work):
            if next(steps, steps) is steps:
                work.remove(steps)


def prepare_kernel(q_ref, g_ref, qgain_ref, kgain_ref, qn_ref, gh_ref, gains_ref):
    qgain = qgain_ref[...]
    for h in range(HEADS):
        columns = slice(h * HEAD_SIZE, (h + 1) * HEAD_SIZE)
        rows = slice(h * ROWS, (h + 1) * ROWS)
        unit, _ = unit_of(q_ref[:, columns].astype(F32))
        qn_ref[rows, :] = (unit * qgain).astype(BF16)
        gh_ref[rows, :] = g_ref[:, columns]
    row = lax.broadcasted_iota(jnp.int32, (8, HEAD_SIZE), 0)
    gains_ref[...] = jnp.where(row == 0, qgain, kgain_ref[...])


def attention_kernel(
    here_ref, qn_ref, g_ref, win_ref, own_ref, gains_ref,
    parts_ref, dqt_ref,
    kn, knt, vals, bias, scores, dprob, probs_b, dscore, dk, dv,
):
    qgain = gains_ref[0:1, :]
    kgain = gains_ref[1:2, :]
    here = here_ref[0]
    key_row = lax.broadcasted_iota(jnp.int32, (ROWS, ROWS), 0)
    query_col = lax.broadcasted_iota(jnp.int32, (ROWS, ROWS), 1)
    seg_q = jnp.broadcast_to(own_ref[2 * ROWS :, :].astype(F32)[0:1, :], (ROWS, ROWS))
    last = 2 * ROWS + EXTRA
    marks = [win_ref[p, 2 * ROWS : last, :].astype(F32)[0:1, :] for p in range(SPAN)]
    marks = jnp.concatenate(marks, axis=0).T
    for p in range(SPAN):
        rows = slice(p * ROWS, (p + 1) * ROWS)
        unit, _ = unit_of(win_ref[p, :ROWS, :].astype(F32))
        normed = (unit * kgain).astype(BF16)
        kn[rows, :] = normed
        knt[:, rows] = normed.T
        vals[rows, :] = win_ref[p, ROWS : 2 * ROWS, :]
        late = jnp.where(here == p, 1, 0) * key_row > query_col
        hidden = jnp.logical_or(marks[:, p : p + 1] != seg_q, late)
        bias[rows, :] = jnp.where(hidden, NEG, 0.0)

    blocks = [slice(p * ROWS, (p + 1) * ROWS) for p in range(SPAN)]
    totals = [None] * GROUPS

    def softmax_steps(n):
        slot, cols = n % 2, slice(n * WIDE, (n + 1) * WIDE)
        top8 = jnp.full((8, WIDE), 2 * NEG, F32)
        for rows in blocks:
            hide = jnp.concatenate([bias[rows, :]] * (WIDE // ROWS), axis=1)
            s = dot_nt(kn[rows, :], qn_ref[cols, :]) + hide
            s = s * EXP2_SCALE
            scores[slot, rows, :] = s
            top8 = jnp.maximum(top8, jnp.max(s.reshape(ROWS // 8, 8, WIDE), axis=0))
            yield
        top = jnp.max(top8, axis=0, keepdims=True)
        total8 = jnp.zeros((8, WIDE), F32)
        for rows in blocks:
            e = jnp.exp2(scores[slot, rows, :] - top)
            scores[slot, rows, :] = e
            total8 = total8 + fold(e)
            yield
        totals[n] = jnp.sum(total8, axis=0, keepdims=True)

    def gradient_steps(n):
        slot, cols = n % 2, slice(n * WIDE, (n + 1) * WIDE)
        inverse_total = 1.0 / totals[n]
        delta8 = jnp.zeros((8, WIDE), F32)
        for rows in blocks:
            prob = scores[slot, rows, :] * inverse_total
            scores[slot, rows, :] = prob
            rounded = prob.astype(BF16)
            probs_b[slot, rows, :] = rounded
            d = dot_nt(vals[rows, :], g_ref[cols, :])
            dprob[rows, :] = d
            delta8 = delta8 + fold(rounded.astype(F32) * d)
            yield
        delta = jnp.sum(delta8, axis=0, keepdims=True)
        values = value_steps(n)
        for rows in blocks:
            next(values, None)
            prob = scores[slot, rows, :]
            dscore[slot, rows, :] = (prob * (dprob[rows, :] - delta)).astype(BF16)
            yield

    def value_steps(n):
        slot, cols = n % 2, slice(n * WIDE, (n + 1) * WIDE)
        for rows in (slice(0, TOKENS // 2), slice(TOKENS // 2, TOKENS)):
            v = dot_nn(probs_b[slot, rows, :], g_ref[cols, :])
            dv[rows, :] = v if n == 0 else dv[rows, :] + v
            yield

    def sum_steps(n):
        slot, cols = n % 2, slice(n * WIDE, (n + 1) * WIDE)
        for rows in (slice(0, TOKENS // 2), slice(TOKENS // 2, TOKENS)):
            k = dot_nn(dscore[slot, rows, :], qn_ref[cols, :])
            dk[rows, :] = k if n == 0 else dk[rows, :] + k
            yield
        dqt_ref[:, cols] = dot_nn(knt[...], dscore[slot]) * SCALE
        yield

    interleave(softmax_steps(0))
    for n in range(GROUPS):
        work = [gradient_steps(n)]
        if n + 1 < GROUPS:
            work.insert(0, softmax_steps(n + 1))
        if n:
            work.append(sum_steps(n - 1))
        interleave(*work)
    interleave(sum_steps(GROUPS - 1))

    ksum = jnp.zeros((8, HEAD_SIZE), F32)
    qsum = jnp.zeros((8, HEAD_SIZE), F32)
    for p, rows in enumerate(blocks):
        unit, _ = unit_of(win_ref[p, :ROWS, :].astype(F32))
        part = dk[rows, :] * SCALE
        ksum = ksum + fold(part * unit)
        qsum = qsum + fold(part * kn[rows, :].astype(F32))
        parts_ref[p, :ROWS, :] = part.astype(BF16)
        parts_ref[p, ROWS : 2 * ROWS, :] = dv[rows, :].astype(BF16)
    q_high, q_low = split(jnp.sum(qsum, axis=0, keepdims=True) / qgain)
    k_high, k_low = split(jnp.sum(ksum, axis=0, keepdims=True))
    row = lax.broadcasted_iota(jnp.int32, (EXTRA, HEAD_SIZE), 0)
    extra = jnp.zeros((EXTRA, HEAD_SIZE), F32)
    for i, x in enumerate((q_high, q_low, k_high, k_low)):
        extra = jnp.where(row == i, x.astype(F32), extra)
    for p in range(SPAN):
        parts_ref[p, 2 * ROWS :, :] = extra.astype(BF16)


def finish_query_kernel(dqt_ref, q_ref, qgain_ref, qgrad_ref):
    qgain = qgain_ref[...]
    for h in range(HEADS):
        columns = slice(h * HEAD_SIZE, (h + 1) * HEAD_SIZE)
        unit, inverse = unit_of(q_ref[:, columns].astype(F32))
        dq = dqt_ref[:, h * ROWS : (h + 1) * ROWS].T
        qgrad_ref[:, columns] = norm_backward(dq, unit, inverse, qgain).astype(BF16)


def combine_kernel(here_ref, parts_ref, own_ref, prev_ref):
    here = here_ref[0]
    for block in (0, 1):
        rows = slice(block * ROWS, (block + 1) * ROWS)
        own = jnp.zeros((ROWS, HEAD_SIZE), F32)
        prev = jnp.zeros((ROWS, HEAD_SIZE), F32)
        for p in range(SPAN):
            part = parts_ref[p, rows, :].astype(F32)
            is_own = p >= here
            own = own + jnp.where(is_own, part, 0.0)
            prev = prev + jnp.where(is_own, 0.0, part)
        own_ref[rows, :] = own
        prev_ref[rows, :] = prev.astype(BF16)


def finish_key_kernel(own_ref, back_ref, key_ref, kgain_ref, kgrad_ref, vgrad_ref):
    unit, inverse = unit_of(key_ref[...].astype(F32))
    dk = own_ref[:ROWS, :] + back_ref[:ROWS, :].astype(F32)
    kgrad_ref[...] = norm_backward(dk, unit, inverse, kgain_ref[...]).astype(BF16)
    vgrad_ref[...] = (own_ref[ROWS:, :] + back_ref[ROWS:, :].astype(F32)).astype(BF16)


VMEM = pl.BlockSpec(memory_space=pltpu.VMEM)
SMEM = pl.BlockSpec(memory_space=pltpu.SMEM)


def call(kernel, name, operands, outs, mib, scratch=(), flops=0, data=0, scalar=False):
    return pl.pallas_call(
        kernel,
        in_specs=[SMEM] * scalar + [VMEM] * (len(operands) - scalar),
        out_specs=[VMEM] * len(outs),
        out_shape=[jax.ShapeDtypeStruct(*out) for out in outs],
        scratch_shapes=list(scratch),
        compiler_params=pltpu.CompilerParams(vmem_limit_bytes=mib * 2**20),
        cost_estimate=pl.CostEstimate(flops=flops, bytes_accessed=data, transcendentals=0),
        name=name,
    )(*operands)


def attention(*operands):
    heads = HEADS * ROWS
    return call(
        attention_kernel, "attention_backward", operands,
        [((SPAN, CHUNK, HEAD_SIZE), BF16), ((HEAD_SIZE, heads), F32)],
        16,
        scratch=[
            pltpu.VMEM((TOKENS, HEAD_SIZE), BF16),
            pltpu.VMEM((HEAD_SIZE, TOKENS), BF16),
            pltpu.VMEM((TOKENS, HEAD_SIZE), BF16),
            pltpu.VMEM((TOKENS, ROWS), F32),
            pltpu.VMEM((2, TOKENS, WIDE), F32),
            pltpu.VMEM((TOKENS, WIDE), F32),
            pltpu.VMEM((2, TOKENS, WIDE), BF16),
            pltpu.VMEM((2, TOKENS, WIDE), BF16),
            pltpu.VMEM((TOKENS, HEAD_SIZE), F32),
            pltpu.VMEM((TOKENS, HEAD_SIZE), F32),
        ],
        flops=4 * 10**9, data=10**7, scalar=True,
    )


def per_device(queries, keys, value, gradient, segments, qgain, kgain):
    here = lax.axis_index(ROW)
    rest = lax.axis_size(REST)
    seq = lax.axis_size(SEQ)
    heads = HEADS * ROWS
    qgain, kgain = qgain.reshape(1, -1), kgain.reshape(1, -1)
    room = jnp.zeros((EXTRA, HEAD_SIZE), BF16)
    own = jnp.concatenate([keys, value, room], axis=0)
    own, segments = lax.optimization_barrier((own, segments))
    own = own.at[2 * ROWS :].set(jnp.broadcast_to(segments.astype(BF16)[None], (EXTRA, ROWS)))
    previous = lax.ppermute(own, SEQ, [(i, (i + SPAN) % seq) for i in range(seq)])
    normed, gradient, gains = call(
        prepare_kernel, "prepare_queries", (queries, gradient, qgain, kgain),
        [((heads, HEAD_SIZE), BF16), ((heads, HEAD_SIZE), BF16), ((8, HEAD_SIZE), F32)],
        4, flops=10**9, data=2 * 10**6,
    )
    previous, normed, gradient, gains = lax.optimization_barrier((previous, normed, gradient, gains))
    is_own = jnp.arange(SPAN) >= here
    outgoing = jnp.where(is_own[:, None, None], own[None], previous[None])
    window = lax.all_to_all(outgoing, ROW, 0, 0)
    place = here.astype(jnp.int32).reshape(1)
    parts, dqt = attention(place, normed, gradient, window, own, gains)
    returned = lax.all_to_all(parts, ROW, 0, 0)
    (qgrad,) = call(
        finish_query_kernel, "finish_queries", (dqt, queries, qgain),
        [((ROWS, heads), BF16)], 4, flops=10**9, data=2 * 10**6,
    )
    factor = 1.0 / math.sqrt(ROWS * seq * HEADS * lax.axis_size("tp"))
    extra = jnp.sum(returned[:, 2 * ROWS : 2 * ROWS + 4].astype(F32), axis=0) * factor
    sums = jnp.broadcast_to((extra[0::2] + extra[1::2])[None], (rest, 2, HEAD_SIZE))
    mine, prev = call(
        combine_kernel, "combine_partials", (place, returned),
        [((2 * ROWS, HEAD_SIZE), F32), ((2 * ROWS, HEAD_SIZE), BF16)],
        4, flops=10**8, data=10**6, scalar=True,
    )
    back = lax.ppermute(prev, SEQ, [((i + SPAN) % seq, i) for i in range(seq)])
    sums = lax.all_to_all(sums, REST, 0, 0)
    kgrad, vgrad = call(
        finish_key_kernel, "finish_keys", (mine, back, keys, kgain),
        [((ROWS, HEAD_SIZE), BF16), ((ROWS, HEAD_SIZE), BF16)], 4, flops=10**8, data=10**6,
    )
    sums = jnp.sum(sums, axis=0)
    return qgrad, kgrad, vgrad, sums[0], sums[1]


def solution(mesh):
    outer, ep, tp = mesh.devices.shape
    fine = Mesh(
        mesh.devices.reshape(2, outer // 4, 2, ep, tp), ("yl", "z", "core", "ep", "tp")
    )
    tokens = P(SEQ, "tp")
    return jax.shard_map(
        per_device,
        mesh=fine,
        in_specs=(tokens, tokens, tokens, tokens, P(SEQ), P(), P()),
        out_specs=(tokens, tokens, tokens, P(), P()),
        check_vma=False,
    )
```
